32 devices in a mesh: groups: 2 (over y), ctx: 4 (over z), head: 4 (over x, core).
Axes of the slice: x: 2, y: 2, z: 4, core: 2. Of those that a mesh axis runs over, the one named last changes fastest.
Arguments:
- queries: bfloat16 [4096, 4096], P(('groups', 'ctx'), 'head'), parts along dimension 0, may hold values from -6 to 6
- key_rows: bfloat16 [4096, 4096], P(('groups', 'ctx'), 'head'), parts along dimension 0, may hold values from -6 to 6
- value_rows: bfloat16 [4096, 4096], P(('groups', 'ctx'), 'head'), parts along dimension 0, may hold values from -6 to 6
- norm_gain: float32 [4096], P('head'), may hold values from 0.1 to 1.9
- out_weight: bfloat16 [4096, 3072], P('head', 'ctx'), may hold values from -0.09375 to 0.09375
- out_grad: bfloat16 [4096, 3072], P(('groups', 'ctx'), 'head'), parts along dimension 0, may hold values from -6 to 6
Outputs:
- mixed: bfloat16 [4096, 3072], P(('groups', 'ctx'), 'head'), parts along dimension 0
- query_grad: bfloat16 [4096, 4096], P(('groups', 'ctx'), 'head'), parts along dimension 0
- key_grad: bfloat16 [4096, 4096], P(('groups', 'ctx'), 'head'), parts along dimension 0
- value_grad: bfloat16 [4096, 4096], P(('groups', 'ctx'), 'head'), parts along dimension 0
The draws below stay inside these ranges and needn't reach their ends.
There are 2 independent parts, one for each index of `groups`. The reference program is written for one: setup_inputs(seed, part) draws one part's arguments, and reference() takes and returns one part's arrays. A program takes and returns all parts, laid end to end along the dimension named above; an argument that names none is the same for every part. Nothing has to cross between parts.
All inputs are finite; a program needn't handle non-finite values.
Results may differ from the reference program's by a relative error of at most 0.009.
Values may be sent and summed in bfloat16 or wider, within the bound.
A program may use at most 64 MiB of HBM per device.

```python
import jax
import jax.numpy as jnp
from jax import lax

D = 3072
HEADS = 32
HD = 128
TOK_DEV = 512
TOKENS = 2048
N_HEAD = 4


def shard_levels(key, shape, shards, low, largest):
    factor_of = 1.0
    for position, blocks in shards:
        steps = jax.random.uniform(jax.random.fold_in(jax.random.fold_in(key, 6), position), (blocks,), jnp.float32, low / len(shards), largest / len(shards))
        factor_of = factor_of * jnp.repeat(jnp.exp(steps), shape[position] // blocks).reshape((-1,) + (1,) * (len(shape) - 1 - position))
    return factor_of


def bell_draw(own_key, dims, deviation, reach, shards=(), kind=jnp.bfloat16):
    gain = shard_levels(own_key, dims, shards, -0.22, 0.18) if shards else 1.0
    entries = jax.random.normal(own_key, dims, jnp.float32) * deviation * gain
    return jnp.minimum(jnp.maximum(entries, -reach), reach).astype(kind)


def setup_inputs(seed: int = 0, part: int = 0) -> dict:
    key_list = jax.random.split(jax.random.key(seed), 7)
    part_keys = jax.random.split(jax.random.fold_in(key_list[6], part), 7)
    return {
        "queries": bell_draw(part_keys[0], (TOKENS, HEADS * HD), 1.0, 6.0, ((0, 4), (1, 4))),
        "key_rows": bell_draw(part_keys[1], (TOKENS, HEADS * HD), 1.0, 6.0, ((0, 4), (1, 4))),
        "value_rows": bell_draw(part_keys[2], (TOKENS, HEADS * HD), 1.0, 6.0, ((0, 4), (1, 4))),
        "norm_gain": jnp.clip(1.0 + 0.18 * jax.random.normal(key_list[3], (HEADS * HD,), jnp.float32), 0.1, 1.9),
        "out_weight": bell_draw(key_list[4], (HEADS * HD, D), (HEADS * HD) ** -0.5, 0.09375, ((0, 4), (1, 4))),
        "out_grad": bell_draw(part_keys[5], (TOKENS, D), 1.0, 6.0, ((0, 4), (1, 4))),
    }


def normed(attended, gain_grid):
    meansq = lax.optimization_barrier(jnp.mean(attended * attended, axis=-1, keepdims=True))
    return attended * lax.rsqrt(meansq + 1e-06) * gain_grid

def reference(queries, key_rows, value_rows, norm_gain, out_weight, out_grad):
    spans = TOKENS // TOK_DEV
    shape4 = (spans, TOK_DEV, HEADS, HD)
    query_all = queries.reshape(shape4)
    key_all = key_rows.reshape(shape4)
    value_all = value_rows.reshape(shape4)
    gain_grid = norm_gain.reshape(HEADS, HD).astype(jnp.float32)
    causal = jnp.tril(jnp.ones((TOK_DEV, TOK_DEV), dtype=bool))
    states = jnp.einsum('clhe,clhf->chef', key_all.astype(jnp.float32), value_all.astype(jnp.float32)).astype(jnp.bfloat16)
    states_wide = states.astype(jnp.float32)
    inclusive = jnp.cumsum(states_wide, axis=0)
    prefix = jnp.concatenate([jnp.zeros_like(states_wide[:1]), inclusive[:-1]], axis=0).astype(jnp.bfloat16)

    def scores_of(query_block, key_block):
        raw = jnp.einsum('lhe,mhe->hlm', query_block.astype(jnp.float32), key_block.astype(jnp.float32))
        return jnp.where(causal, raw, 0.0).astype(jnp.bfloat16)

    def forward_block(packed):
        query_block, key_block, value_block, prefix_block = packed
        scores = scores_of(query_block, key_block)
        inter = jnp.einsum('lhe,hef->lhf', query_block.astype(jnp.float32), prefix_block.astype(jnp.float32))
        intra = jnp.einsum('hlm,mhf->lhf', scores.astype(jnp.float32), value_block.astype(jnp.float32))
        return inter + intra
    attended = lax.map(forward_block, (query_all, key_all, value_all, prefix))
    hidden = normed(attended, gain_grid).astype(jnp.bfloat16).reshape(TOKENS, HEADS * HD)
    group = HEADS * HD // N_HEAD
    running = jnp.zeros((TOKENS, D), jnp.float32)
    for index in range(N_HEAD):
        partial_value = jnp.dot(hidden[:, index * group:(index + 1) * group], out_weight[index * group:(index + 1) * group], preferred_element_type=jnp.float32)
        running = running + lax.optimization_barrier(partial_value.astype(jnp.bfloat16)).astype(jnp.float32)
    mixed = running.astype(jnp.bfloat16)
    grad_hidden = jnp.dot(out_grad, out_weight.T, preferred_element_type=jnp.float32).reshape(shape4)
    _, pullback = jax.vjp(lambda values_in: normed(values_in, gain_grid), attended)
    grad_attended = pullback(grad_hidden)[0].astype(jnp.bfloat16)
    grad_states = jnp.einsum('clhe,clhf->chef', query_all.astype(jnp.float32), grad_attended.astype(jnp.float32)).astype(jnp.bfloat16).astype(jnp.float32)
    reverse_sum = jnp.cumsum(grad_states[::-1], axis=0)[::-1]
    suffix = jnp.concatenate([reverse_sum[1:], jnp.zeros_like(grad_states[:1])], axis=0).astype(jnp.bfloat16)

    def backward_block(packed):
        query_block, key_block, value_block, prefix_block, suffix_block, grad_block = packed
        query_wide = query_block.astype(jnp.float32)
        key_wide = key_block.astype(jnp.float32)
        value_wide = value_block.astype(jnp.float32)
        grad_wide = grad_block.astype(jnp.float32)
        prefix_wide = prefix_block.astype(jnp.float32)
        suffix_wide = suffix_block.astype(jnp.float32)
        scores = scores_of(query_block, key_block).astype(jnp.float32)
        grad_scores = jnp.where(causal, jnp.einsum('lhf,mhf->hlm', grad_wide, value_wide), 0.0).astype(jnp.bfloat16).astype(jnp.float32)
        query_part = jnp.einsum('hlm,mhe->lhe', grad_scores, key_wide) + jnp.einsum('lhf,hef->lhe', grad_wide, prefix_wide)
        key_part = jnp.einsum('hlm,lhe->mhe', grad_scores, query_wide) + jnp.einsum('mhf,hef->mhe', value_wide, suffix_wide)
        value_part = jnp.einsum('hlm,lhf->mhf', scores, grad_wide) + jnp.einsum('mhe,hef->mhf', key_wide, suffix_wide)
        return (query_part.astype(jnp.bfloat16), key_part.astype(jnp.bfloat16), value_part.astype(jnp.bfloat16))
    query_grad, key_grad, value_grad = lax.map(backward_block, (query_all, key_all, value_all, prefix, suffix, grad_attended))
    flat = (TOKENS, HEADS * HD)
    return (mixed, query_grad.reshape(flat), key_grad.reshape(flat), value_grad.reshape(flat))
```

```python
import jax
import jax.numpy as jnp
from jax import lax
from jax.experimental import pallas as pl
from jax.experimental.pallas import tpu as pltpu
from jax.sharding import PartitionSpec as P

HD = 128


def normed(attended, gain_grid):
    meansq = jnp.mean(attended * attended, axis=-1, keepdims=True)
    return attended * lax.rsqrt(meansq + 1e-06) * gain_grid


def on_device(queries, key_rows, value_rows, norm_gain, out_weight, out_grad):
    rows = queries.shape[0]
    heads_here = queries.shape[1] // HD
    query_loc = queries.reshape(rows, heads_here, HD)
    key_loc = key_rows.reshape(rows, heads_here, HD)
    value_loc = value_rows.reshape(rows, heads_here, HD)
    gain_grid = norm_gain.reshape(heads_here, HD)
    position = lax.axis_index("ctx")
    blocks = lax.axis_size("ctx")
    order = jnp.arange(blocks)
    causal = jnp.tril(jnp.ones((rows, rows), dtype=bool))
    states = jnp.einsum(
        "lhe,lhf->hef", key_loc, value_loc, preferred_element_type=jnp.float32
    ).astype(jnp.bfloat16)
    gathered = lax.all_gather(states[None], "ctx", axis=0, tiled=True)
    earlier_mask = order < position
    prefix = jnp.sum(
        jnp.where(earlier_mask[:, None, None, None], gathered.astype(jnp.float32), 0.0), axis=0
    )
    prefix_low = prefix.astype(jnp.bfloat16)
    raw_scores = jnp.einsum("lhe,mhe->hlm", query_loc, key_loc, preferred_element_type=jnp.float32)
    scores = jnp.where(causal, raw_scores, 0.0).astype(jnp.bfloat16)
    attended = jnp.einsum("lhe,hef->lhf", query_loc, prefix_low, preferred_element_type=jnp.float32)
    attended = attended + jnp.einsum(
        "hlm,mhf->lhf", scores, value_loc, preferred_element_type=jnp.float32
    )
    hidden = normed(attended, gain_grid).astype(jnp.bfloat16).reshape(rows, heads_here * HD)
    full_weight = lax.all_gather(out_weight, "ctx", axis=1, tiled=True)
    partial_value = jnp.dot(hidden, full_weight, preferred_element_type=jnp.float32)
    mixed = lax.psum_scatter(
        partial_value.astype(jnp.bfloat16), "head", scatter_dimension=1, tiled=True
    )
    grad_cols = lax.all_gather(out_grad, "head", axis=1, tiled=True)
    grad_hidden = lax.dot_general(
        grad_cols, full_weight, (((1,), (1,)), ((), ())), preferred_element_type=jnp.float32
    )
    grad_hidden = grad_hidden.reshape(rows, heads_here, HD)
    _, pullback = jax.vjp(lambda values_in: normed(values_in, gain_grid), attended)
    grad_attended = pullback(grad_hidden)[0].astype(jnp.bfloat16)
    grad_state = jnp.einsum(
        "lhe,lhf->hef", query_loc, grad_attended, preferred_element_type=jnp.float32
    ).astype(jnp.bfloat16)
    gathered_grads = lax.all_gather(grad_state[None], "ctx", axis=0, tiled=True)
    later_mask = order > position
    suffix = jnp.sum(
        jnp.where(later_mask[:, None, None, None], gathered_grads.astype(jnp.float32), 0.0), axis=0
    )
    suffix_low = suffix.astype(jnp.bfloat16)
    raw_grad = jnp.einsum(
        "lhf,mhf->hlm", grad_attended, value_loc, preferred_element_type=jnp.float32
    )
    grad_scores = jnp.where(causal, raw_grad, 0.0).astype(jnp.bfloat16)
    query_grad = jnp.einsum(
        "hlm,mhe->lhe", grad_scores, key_loc, preferred_element_type=jnp.float32
    )
    query_grad = query_grad + jnp.einsum(
        "lhf,hef->lhe", grad_attended, prefix_low, preferred_element_type=jnp.float32
    )
    key_grad = jnp.einsum(
        "hlm,lhe->mhe", grad_scores, query_loc, preferred_element_type=jnp.float32
    )
    key_grad = key_grad + jnp.einsum(
        "mhf,hef->mhe", value_loc, suffix_low, preferred_element_type=jnp.float32
    )
    value_grad = jnp.einsum(
        "hlm,lhf->mhf", scores, grad_attended, preferred_element_type=jnp.float32
    )
    value_grad = value_grad + jnp.einsum(
        "mhe,hef->mhf", key_loc, suffix_low, preferred_element_type=jnp.float32
    )
    flat = (rows, heads_here * HD)
    return (
        mixed,
        query_grad.reshape(flat).astype(jnp.bfloat16),
        key_grad.reshape(flat).astype(jnp.bfloat16),
        value_grad.reshape(flat).astype(jnp.bfloat16),
    )


MESH_OF_KERNEL = {"groups": 2, "ctx": 4, "head": 4}
PIECES = 3
SPANS = 4
F32 = jnp.float32
BF16 = jnp.bfloat16
NN = (((1,), (0,)), ((), ()))
NT = (((1,), (1,)), ((), ()))
TN = (((0,), (0,)), ((), ()))


def mul(a, b, dims):
    return lax.dot_general(a, b, dims, preferred_element_type=F32)


def fused_kernel(
    q_ref, k_ref, v_ref, gain_ref, w_ref, og_ref,
    mixed_ref, dq_ref, dk_ref, dv_ref,
    wall, ogall, att, gh, scores, hid, dout,
    pacc, csend, cin, xsend, xin, sbuf, pbuf, psend, rbuf, gbuf, gsend,
    local_sem, up_sem, down_sem, z_sem, ysend_sem, yrecv_sem, ogsend_sem, ogrecv_sem,
    psend_sem, precv_sem, rsend_sem, rrecv_sem, csend_sem, crecv_sem, xsend_sem, xrecv_sem,
):
    rows = q_ref.shape[0]
    heads = q_ref.shape[1] // HD
    half_cols = wall.shape[3]
    piece = half_cols // PIECES
    part = heads // SPANS
    g = lax.axis_index("groups")
    z = lax.axis_index("ctx")
    h = lax.axis_index("head")
    last = 3
    x, c = h // 2, h % 2
    to_up, to_down = {"ctx": z + 1}, {"ctx": z - 1}
    to_y = {"groups": 1 - g}
    to_core = {"head": x * 2 + 1 - c}
    to_x = {"head": (1 - x) * 2 + c}

    def remote(src, dst, send, recv, to):
        return pltpu.make_async_remote_copy(
            src_ref=src, dst_ref=dst, send_sem=send, recv_sem=recv,
            device_id=to, device_id_type=pl.DeviceIdType.MESH,
        )

    barrier = pltpu.get_barrier_semaphore()

    def greet(to):
        pl.semaphore_signal(barrier, inc=1, device_id=to, device_id_type=pl.DeviceIdType.MESH)

    greet(to_y)
    greet(to_core)
    greet(to_x)
    pl.when(z < last)(lambda: greet(to_up))
    pl.when(z > 0)(lambda: greet(to_down))
    pl.semaphore_wait(barrier, 3 + jnp.where(z < last, 1, 0) + jnp.where(z > 0, 1, 0))

    def cols(index, width):
        return pl.ds(pl.multiple_of(index * width, HD), width)

    def head_cols(index):
        return cols(index, HD)

    def w_piece(k, half, j):
        return wall.at[k, half, :, cols(j, piece)]

    def own_piece(j):
        return w_ref.at[:, cols(g * PIECES + j, piece)]

    def z_copy(src, k, j, send, to):
        return remote(src, w_piece(k, g, j), send.at[k, j], z_sem.at[k, j], to)

    def up_copy(k, j, src=None):
        return z_copy(w_piece(k, g, j) if src is None else src, k, j, up_sem, to_up)

    def down_copy(k, j, src=None):
        return z_copy(w_piece(k, g, j) if src is None else src, k, j, down_sem, to_down)

    def y_copy(k, half, j):
        return remote(w_piece(k, half, j), w_piece(k, half, j), ysend_sem.at[k, j], yrecv_sem.at[k, j], to_y)

    def og_copy(slot, index, src, to):
        return remote(src, ogall.at[slot], ogsend_sem.at[index], ogrecv_sem.at[index], to)

    og_core = og_copy(h, 0, og_ref, to_core)
    og_x = og_copy(h, 1, og_ref, to_x)
    across = (1 - x) * 2 + c
    og_forward = og_copy(across, 2, ogall.at[across], to_core)
    own_og = pltpu.make_async_copy(og_ref, ogall.at[h], local_sem.at[2])
    own_w = [
        pltpu.make_async_copy(w_ref.at[:, i * half_cols:(i + 1) * half_cols], wall.at[z, i], local_sem.at[i])
        for i in range(2)
    ]

    for j in range(PIECES):
        pl.when(z < last)(lambda j=j: up_copy(z, j, own_piece(j)).start())
        pl.when(z > 0)(lambda j=j: down_copy(z, j, own_piece(j)).start())
    og_x.start()
    og_core.start()
    own_og.start()
    for copy in own_w:
        copy.start()

    def span(ref, i):
        return ref.at[pl.ds(i * part, part)]

    def p_copy(i, src):
        return remote(span(src, i), span(pbuf, i), psend_sem.at[i], precv_sem.at[i], to_up)

    def r_copy(i, src):
        return remote(span(src, i), span(gbuf, i), rsend_sem.at[i], rrecv_sem.at[i], to_down)

    def state_step(i, carry):
        sbuf[i] = mul(k_ref[:, head_cols(i)], v_ref[:, head_cols(i)], TN).astype(BF16)
        return carry

    lax.fori_loop(0, heads, state_step, 0)

    @pl.when(z == 0)
    def _():
        for i in range(SPANS):
            p_copy(i, sbuf).start()
        pbuf[...] = jnp.zeros_like(pbuf)

    causal = lax.broadcasted_iota(jnp.int32, (rows, rows), 0) >= lax.broadcasted_iota(jnp.int32, (rows, rows), 1)

    def score_step(i, carry):
        own = jnp.where(causal, mul(q_ref[:, head_cols(i)], k_ref[:, head_cols(i)], NT), 0.0).astype(BF16)
        scores[i] = own
        att[:, head_cols(i)] = mul(own, v_ref[:, head_cols(i)], NN)
        return carry

    lax.fori_loop(0, heads, score_step, 0)

    def pass_on(s):
        for j in range(PIECES):
            @pl.when((s > 0) & (z - s >= 0))
            def _():
                k = z - s
                up_copy(k, j).wait_recv()
                y_copy(k, g, j).start()
                pl.when(z < last)(lambda: up_copy(k, j).start())

            @pl.when((s > 0) & (z + s <= last))
            def _():
                k = z + s
                down_copy(k, j).wait_recv()
                y_copy(k, g, j).start()
                pl.when(z > 0)(lambda: down_copy(k, j).start())

    og_copy(across, 1, og_ref, to_x).wait_recv()
    og_forward.start()
    pass_on(1)

    @pl.when(z > 0)
    def _():
        for i in range(SPANS):
            p_copy(i, psend).wait_recv()

            @pl.when(z < last)
            def _():
                at = pl.ds(i * part, part)
                psend[at] = (sbuf[at].astype(F32) + pbuf[at].astype(F32)).astype(BF16)
                p_copy(i, psend).start()

    def hidden_step(i, carry):
        at = head_cols(i)
        whole = att[:, at] + mul(q_ref[:, at], pbuf[i], NN)
        att[:, at] = whole
        scale = lax.rsqrt(jnp.mean(whole * whole, axis=-1, keepdims=True) + 1e-06)
        hid[:, at] = (whole * scale * gain_ref[:, at]).astype(BF16)
        return carry

    lax.fori_loop(0, heads, hidden_step, 0)

    own_og.wait()
    for copy in own_w:
        copy.wait()
    og_core.wait_recv()
    og_forward.wait_recv()
    gh[...] = jnp.zeros_like(gh)

    def core_copy(xk, half):
        return remote(csend.at[xk, half], cin.at[xk, half], csend_sem.at[xk, half], crecv_sem.at[xk, half], to_core)

    def x_copy(half):
        return remote(xsend.at[half], xin.at[half], xsend_sem.at[half], xrecv_sem.at[half], to_x)

    def work(k, half):
        xk, ck = k // 2, k % 2
        weight = wall[k, half]
        term = mul(hid[...], weight, NN)

        @pl.when(ck != c)
        def _():
            csend[xk, half] = term.astype(BF16)
            core_copy(xk, half).start()

        @pl.when(ck == c)
        def _():
            pacc[xk, half] = term

        gh[...] += mul(ogall[k, :, cols(half, half_cols)], weight, NT)

        @pl.when(ck == c)
        def _():
            core_copy(xk, half).wait_recv()
            both = pacc[xk, half] + cin[xk, half].astype(F32)

            @pl.when(xk == x)
            def _():
                pacc[xk, half] = both

            @pl.when(xk != x)
            def _():
                xsend[half] = both.astype(BF16)
                x_copy(half).start()

    def ring_step(s, carry):
        pl.when(s > 1)(lambda: pass_on(s))

        def sub_step(i, inner):
            above, late = i % 2, i // 2
            k = jnp.where(above == 0, z - s, z + s)
            half = jnp.where(late == 0, g, 1 - g)

            @pl.when((k >= 0) & (k <= last) & ((s > 0) | (above == 0)))
            def _():
                @pl.when((late == 1) & (s > 0))
                def _():
                    for j in range(PIECES):
                        y_copy(k, half, j).wait_recv()
                work(k, half)
            return inner

        lax.fori_loop(0, 4, sub_step, 0)
        return carry

    lax.fori_loop(0, 4, ring_step, 0)

    def norm_step(i, carry):
        at = head_cols(i)
        whole = att[:, at]
        scale = lax.rsqrt(jnp.mean(whole * whole, axis=-1, keepdims=True) + 1e-06)
        scaled = gh[:, at] * gain_ref[:, at]
        inner = jnp.mean(scaled * whole, axis=-1, keepdims=True) * scale * scale
        grad = ((scaled - whole * inner) * scale).astype(BF16)
        dout[:, at] = grad
        rbuf[i] = mul(q_ref[:, at], grad, TN).astype(BF16)
        return carry

    lax.fori_loop(0, heads, norm_step, 0)

    @pl.when(z == last)
    def _():
        for i in range(SPANS):
            r_copy(i, rbuf).start()
        gbuf[...] = jnp.zeros_like(gbuf)

    def grad_step(i, carry):
        at = head_cols(i)
        grad = dout[:, at]
        back = jnp.where(causal, mul(grad, v_ref[:, at], NT), 0.0).astype(BF16)
        dq_ref[:, at] = (mul(back, k_ref[:, at], NN) + mul(grad, pbuf[i], NT)).astype(BF16)
        att[:, at] = mul(back, q_ref[:, at], TN)
        gh[:, at] = mul(scores[i], grad, TN)
        return carry

    lax.fori_loop(0, heads, grad_step, 0)

    @pl.when(z < last)
    def _():
        for i in range(SPANS):
            r_copy(i, gsend).wait_recv()

            @pl.when(z > 0)
            def _():
                at = pl.ds(i * part, part)
                gsend[at] = (rbuf[at].astype(F32) + gbuf[at].astype(F32)).astype(BF16)
                r_copy(i, gsend).start()

    def last_step(i, carry):
        at = head_cols(i)
        dk_ref[:, at] = (att[:, at] + mul(v_ref[:, at], gbuf[i], NT)).astype(BF16)
        dv_ref[:, at] = (gh[:, at] + mul(k_ref[:, at], gbuf[i], NN)).astype(BF16)
        return carry

    lax.fori_loop(0, heads, last_step, 0)

    for half in range(2):
        x_copy(half).wait_recv()
        mixed_ref[:, half * half_cols:(half + 1) * half_cols] = (
            pacc[x, half] + xin[half].astype(F32)
        ).astype(BF16)

    og_core.wait_send()
    og_x.wait_send()
    og_forward.wait_send()
    for half in range(2):
        x_copy(half).wait_send()
        for xk in range(2):
            core_copy(xk, half).wait_send()
    for i in range(SPANS):
        pl.when(z < last)(lambda i=i: p_copy(i, sbuf).wait_send())
        pl.when(z > 0)(lambda i=i: r_copy(i, rbuf).wait_send())
    for k in range(4):
        for j in range(PIECES):
            pl.when((z >= k) & (z < last))(lambda k=k, j=j: up_copy(k, j).wait_send())
            pl.when((z <= k) & (z > 0))(lambda k=k, j=j: down_copy(k, j).wait_send())
            pl.when(z != k)(lambda k=k, j=j: y_copy(k, g, j).wait_send())


def on_device_fused(queries, key_rows, value_rows, norm_gain, out_weight, out_grad):
    rows, width = queries.shape
    heads = width // HD
    share = out_weight.shape[1]
    half = share // 2
    inside = pl.BlockSpec(memory_space=pltpu.VMEM)
    anywhere = pl.BlockSpec(memory_space=pl.ANY)
    grid_of = jax.ShapeDtypeStruct((rows, width), BF16)
    dma = pltpu.SemaphoreType.DMA
    states = pltpu.VMEM((heads, HD, HD), BF16)
    return pl.pallas_call(
        fused_kernel,
        out_shape=(jax.ShapeDtypeStruct((rows, share), BF16), grid_of, grid_of, grid_of),
        in_specs=[inside] * 4 + [anywhere] * 2,
        out_specs=(inside,) * 4,
        scratch_shapes=[
            pltpu.VMEM((4, 2, width, half), BF16),
            pltpu.VMEM((4, rows, share), BF16),
            pltpu.VMEM((rows, width), F32),
            pltpu.VMEM((rows, width), F32),
            pltpu.VMEM((heads, rows, rows), BF16),
            pltpu.VMEM((rows, width), BF16),
            pltpu.VMEM((rows, width), BF16),
            pltpu.VMEM((2, 2, rows, half), F32),
            pltpu.VMEM((2, 2, rows, half), BF16),
            pltpu.VMEM((2, 2, rows, half), BF16),
            pltpu.VMEM((2, rows, half), BF16),
            pltpu.VMEM((2, rows, half), BF16),
            states, states, states, states, states, states,
            dma((3,)),
            dma((4, PIECES)), dma((4, PIECES)), dma((4, PIECES)), dma((4, PIECES)), dma((4, PIECES)),
            dma((3,)), dma((3,)),
            dma((SPANS,)), dma((SPANS,)), dma((SPANS,)), dma((SPANS,)),
            dma((2, 2)), dma((2, 2)), dma((2,)), dma((2,)),
        ],
        compiler_params=pltpu.CompilerParams(
            collective_id=0, has_side_effects=True, vmem_limit_bytes=56 * 1024 * 1024
        ),
        cost_estimate=pl.CostEstimate(flops=12 * 10**9, bytes_accessed=10**7, transcendentals=rows * heads),
    )(queries, key_rows, value_rows, norm_gain.reshape(1, width), out_weight, out_grad)


def solution(mesh):
    placed = (
        P(("groups", "ctx"), "head"),
        P(("groups", "ctx"), "head"),
        P(("groups", "ctx"), "head"),
        P("head"),
        P("head", "ctx"),
        P(("groups", "ctx"), "head"),
    )
    fused = all(mesh.shape[name] == size for name, size in MESH_OF_KERNEL.items())
    return jax.shard_map(
        on_device_fused if fused else on_device,
        mesh=mesh,
        in_specs=placed,
        out_specs=(
            P(("groups", "ctx"), "head"),
            P(("groups", "ctx"), "head"),
            P(("groups", "ctx"), "head"),
            P(("groups", "ctx"), "head"),
        ),
        check_vma=False,
    )
```

```python
import jax
import jax.numpy as jnp
from jax import lax
from jax.experimental import pallas as pl
from jax.experimental.pallas import tpu as pltpu
from jax.sharding import PartitionSpec as P

HD = 128


def normed(attended, gain_grid):
    meansq = jnp.mean(attended * attended, axis=-1, keepdims=True)
    return attended * lax.rsqrt(meansq + 1e-06) * gain_grid


def on_device(queries, key_rows, value_rows, norm_gain, out_weight, out_grad):
    rows = queries.shape[0]
    heads_here = queries.shape[1] // HD
    query_loc = queries.reshape(rows, heads_here, HD)
    key_loc = key_rows.reshape(rows, heads_here, HD)
    value_loc = value_rows.reshape(rows, heads_here, HD)
    gain_grid = norm_gain.reshape(heads_here, HD)
    position = lax.axis_index("ctx")
    blocks = lax.axis_size("ctx")
    order = jnp.arange(blocks)
    causal = jnp.tril(jnp.ones((rows, rows), dtype=bool))
    states = jnp.einsum(
        "lhe,lhf->hef", key_loc, value_loc, preferred_element_type=jnp.float32
    ).astype(jnp.bfloat16)
    gathered = lax.all_gather(states[None], "ctx", axis=0, tiled=True)
    earlier_mask = order < position
    prefix = jnp.sum(
        jnp.where(earlier_mask[:, None, None, None], gathered.astype(jnp.float32), 0.0), axis=0
    )
    prefix_low = prefix.astype(jnp.bfloat16)
    raw_scores = jnp.einsum("lhe,mhe->hlm", query_loc, key_loc, preferred_element_type=jnp.float32)
    scores = jnp.where(causal, raw_scores, 0.0).astype(jnp.bfloat16)
    attended = jnp.einsum("lhe,hef->lhf", query_loc, prefix_low, preferred_element_type=jnp.float32)
    attended = attended + jnp.einsum(
        "hlm,mhf->lhf", scores, value_loc, preferred_element_type=jnp.float32
    )
    hidden = normed(attended, gain_grid).astype(jnp.bfloat16).reshape(rows, heads_here * HD)
    full_weight = lax.all_gather(out_weight, "ctx", axis=1, tiled=True)
    partial_value = jnp.dot(hidden, full_weight, preferred_element_type=jnp.float32)
    mixed = lax.psum_scatter(
        partial_value.astype(jnp.bfloat16), "head", scatter_dimension=1, tiled=True
    )
    grad_cols = lax.all_gather(out_grad, "head", axis=1, tiled=True)
    grad_hidden = lax.dot_general(
        grad_cols, full_weight, (((1,), (1,)), ((), ())), preferred_element_type=jnp.float32
    )
    grad_hidden = grad_hidden.reshape(rows, heads_here, HD)
    _, pullback = jax.vjp(lambda values_in: normed(values_in, gain_grid), attended)
    grad_attended = pullback(grad_hidden)[0].astype(jnp.bfloat16)
    grad_state = jnp.einsum(
        "lhe,lhf->hef", query_loc, grad_attended, preferred_element_type=jnp.float32
    ).astype(jnp.bfloat16)
    gathered_grads = lax.all_gather(grad_state[None], "ctx", axis=0, tiled=True)
    later_mask = order > position
    suffix = jnp.sum(
        jnp.where(later_mask[:, None, None, None], gathered_grads.astype(jnp.float32), 0.0), axis=0
    )
    suffix_low = suffix.astype(jnp.bfloat16)
    raw_grad = jnp.einsum(
        "lhf,mhf->hlm", grad_attended, value_loc, preferred_element_type=jnp.float32
    )
    grad_scores = jnp.where(causal, raw_grad, 0.0).astype(jnp.bfloat16)
    query_grad = jnp.einsum(
        "hlm,mhe->lhe", grad_scores, key_loc, preferred_element_type=jnp.float32
    )
    query_grad = query_grad + jnp.einsum(
        "lhf,hef->lhe", grad_attended, prefix_low, preferred_element_type=jnp.float32
    )
    key_grad = jnp.einsum(
        "hlm,lhe->mhe", grad_scores, query_loc, preferred_element_type=jnp.float32
    )
    key_grad = key_grad + jnp.einsum(
        "mhf,hef->mhe", value_loc, suffix_low, preferred_element_type=jnp.float32
    )
    value_grad = jnp.einsum(
        "hlm,lhf->mhf", scores, grad_attended, preferred_element_type=jnp.float32
    )
    value_grad = value_grad + jnp.einsum(
        "mhe,hef->mhf", key_loc, suffix_low, preferred_element_type=jnp.float32
    )
    flat = (rows, heads_here * HD)
    return (
        mixed,
        query_grad.reshape(flat).astype(jnp.bfloat16),
        key_grad.reshape(flat).astype(jnp.bfloat16),
        value_grad.reshape(flat).astype(jnp.bfloat16),
    )


MESH_OF_KERNEL = {"groups": 2, "ctx": 4, "head": 4}
PIECES = 3
SPANS = 4
F32 = jnp.float32
BF16 = jnp.bfloat16
NN = (((1,), (0,)), ((), ()))
NT = (((1,), (1,)), ((), ()))
TN = (((0,), (0,)), ((), ()))


def mul(a, b, dims):
    return lax.dot_general(a, b, dims, preferred_element_type=F32)


def fused_kernel(
    q_ref, k_ref, v_ref, gain_ref, w_ref, og_ref,
    mixed_ref, dq_ref, dk_ref, dv_ref,
    wall, ogall, att, gh, scores, hid, dout,
    macc, csend, cin, xsend, xin, sbuf, pbuf, psend, rbuf, gbuf, gsend,
    local_sem, up_sem, down_sem, z_sem, ysend_sem, yrecv_sem, ogsend_sem, ogrecv_sem,
    psend_sem, precv_sem, rsend_sem, rrecv_sem, csend_sem, crecv_sem, xsend_sem, xrecv_sem,
):
    rows = q_ref.shape[0]
    heads = q_ref.shape[1] // HD
    half_cols = w_ref.shape[1] // 2
    piece = half_cols // PIECES
    band = wall.shape[2]
    mid = heads // 2
    part = heads // SPANS
    g = lax.axis_index("groups")
    z = lax.axis_index("ctx")
    h = lax.axis_index("head")
    last = 3
    x, c = h // 2, h % 2
    to_up, to_down = {"ctx": z + 1}, {"ctx": z - 1}
    to_y = {"groups": 1 - g}
    to_core = {"head": x * 2 + 1 - c}
    to_x = {"head": (1 - x) * 2 + c}

    def remote(src, dst, send, recv, to):
        return pltpu.make_async_remote_copy(
            src_ref=src, dst_ref=dst, send_sem=send, recv_sem=recv,
            device_id=to, device_id_type=pl.DeviceIdType.MESH,
        )

    barrier = pltpu.get_barrier_semaphore()

    def greet(to):
        pl.semaphore_signal(barrier, inc=1, device_id=to, device_id_type=pl.DeviceIdType.MESH)

    greet(to_y)
    greet(to_core)
    greet(to_x)
    pl.when(z < last)(lambda: greet(to_up))
    pl.when(z > 0)(lambda: greet(to_down))
    pl.semaphore_wait(barrier, 3 + jnp.where(z < last, 1, 0) + jnp.where(z > 0, 1, 0))

    def cols(index, width):
        if isinstance(index, int):
            return slice(index * width, (index + 1) * width)
        return pl.ds(pl.multiple_of(index * width, HD), width)

    def head_cols(index):
        return cols(index, HD)

    def w_piece(k, b, half, j):
        return wall.at[k, b, :, cols(half * PIECES + j, piece)]

    def own_piece(b, j):
        return w_ref.at[b * band:(b + 1) * band, cols(g * PIECES + j, piece)]

    def z_copy(src, k, b, j, send, to):
        return remote(src, w_piece(k, b, g, j), send.at[k, b, j], z_sem.at[k, b, j], to)

    def up_copy(k, b, j, src=None):
        return z_copy(w_piece(k, b, g, j) if src is None else src, k, b, j, up_sem, to_up)

    def down_copy(k, b, j, src=None):
        return z_copy(w_piece(k, b, g, j) if src is None else src, k, b, j, down_sem, to_down)

    def y_copy(k, b, half, j):
        return remote(
            w_piece(k, b, half, j), w_piece(k, b, half, j), ysend_sem.at[k, b, j], yrecv_sem.at[k, b, j], to_y
        )

    def og_copy(slot, index, src, to):
        return remote(src, ogall.at[slot], ogsend_sem.at[index], ogrecv_sem.at[index], to)

    og_core = og_copy(h, 0, og_ref, to_core)
    og_x = og_copy(h, 1, og_ref, to_x)
    across = (1 - x) * 2 + c
    og_forward = og_copy(across, 2, ogall.at[across], to_core)
    own_og = pltpu.make_async_copy(og_ref, ogall.at[h], local_sem.at[2])
    own_w = [
        pltpu.make_async_copy(w_ref.at[i * band:(i + 1) * band], wall.at[z, i], local_sem.at[i])
        for i in range(2)
    ]

    def send_own(b):
        for j in range(PIECES):
            pl.when(z < last)(lambda j=j: up_copy(z, b, j, own_piece(b, j)).start())
            pl.when(z > 0)(lambda j=j: down_copy(z, b, j, own_piece(b, j)).start())

    def for_heads(low, high, step):
        for i in range(low, high):
            step(i)

    send_own(0)
    og_x.start()
    og_core.start()
    own_og.start()
    for copy in own_w:
        copy.start()

    def span(ref, i):
        return ref.at[pl.ds(i * part, part)]

    def p_copy(i, src):
        return remote(span(src, i), span(pbuf, i), psend_sem.at[i], precv_sem.at[i], to_up)

    def r_copy(i, src):
        return remote(span(src, i), span(gbuf, i), rsend_sem.at[i], rrecv_sem.at[i], to_down)

    def state_step(i):
        sbuf[i] = mul(k_ref[:, head_cols(i)], v_ref[:, head_cols(i)], TN).astype(BF16)

    for_heads(0, heads, state_step)

    @pl.when(z == 0)
    def _():
        for i in range(SPANS):
            p_copy(i, sbuf).start()
        pbuf[...] = jnp.zeros_like(pbuf)

    block = rows // 2
    causal = lax.broadcasted_iota(jnp.int32, (block, block), 0) >= lax.broadcasted_iota(jnp.int32, (block, block), 1)
    early, late = slice(0, block), slice(block, rows)

    def masked(left, right):
        first = jnp.where(causal, mul(left[:block], right[:block], NT), 0.0).astype(BF16)
        cross = mul(left[block:], right[:block], NT).astype(BF16)
        second = jnp.where(causal, mul(left[block:], right[block:], NT), 0.0).astype(BF16)
        return first, jnp.concatenate([cross, second], axis=1)

    def score_step(i):
        at = head_cols(i)
        first, below = masked(q_ref[:, at], k_ref[:, at])
        scores[i, early, early] = first
        scores[i, late, :] = below
        att[early, at] = mul(first, v_ref[early, at], NN)
        att[late, at] = mul(below, v_ref[:, at], NN)

    def pass_on(b, s):
        for j in range(PIECES):
            @pl.when(z - s >= 0)
            def _():
                k = z - s
                up_copy(k, b, j).wait_recv()
                y_copy(k, b, g, j).start()
                pl.when(z < last)(lambda: up_copy(k, b, j).start())

            @pl.when(z + s <= last)
            def _():
                k = z + s
                down_copy(k, b, j).wait_recv()
                y_copy(k, b, g, j).start()
                pl.when(z > 0)(lambda: down_copy(k, b, j).start())

    for_heads(0, mid, score_step)
    pass_on(0, 1)
    for_heads(mid, heads, score_step)
    og_copy(across, 1, og_ref, to_x).wait_recv()
    og_forward.start()
    pass_on(0, 2)
    send_own(1)

    @pl.when(z > 0)
    def _():
        for i in range(SPANS):
            p_copy(i, psend).wait_recv()

            @pl.when(z < last)
            def _():
                at = pl.ds(i * part, part)
                psend[at] = (sbuf[at].astype(F32) + pbuf[at].astype(F32)).astype(BF16)
                p_copy(i, psend).start()

    def hidden_step(i):
        at = head_cols(i)
        whole = att[:, at] + mul(q_ref[:, at], pbuf[i], NN)
        att[:, at] = whole
        scale = lax.rsqrt(jnp.mean(whole * whole, axis=-1, keepdims=True) + 1e-06)
        hid[:, at] = (whole * scale * gain_ref[:, at]).astype(BF16)

    for_heads(0, heads, hidden_step)

    own_og.wait()
    for copy in own_w:
        copy.wait()
    og_core.wait_recv()
    og_forward.wait_recv()

    def core_copy(xk):
        return remote(csend.at[xk], cin.at[xk], csend_sem.at[xk], crecv_sem.at[xk], to_core)

    x_copy = remote(xsend, xin, xsend_sem.at[0], xrecv_sem.at[0], to_x)

    def work(k, b, opening):
        lanes = slice(b * band, (b + 1) * band)
        xk, ck = k // 2, k % 2
        weight = wall[k, b]
        term = mul(hid[:, lanes], weight, NN)
        if b == 0:
            macc[k] = term
        else:
            term = macc[k] + term

            @pl.when(ck != c)
            def _():
                csend[xk] = term.astype(BF16)
                core_copy(xk).start()

            @pl.when(ck == c)
            def _():
                macc[k] = term

        back = mul(ogall[k], weight, NT)
        gh[:, lanes] = back if opening else gh[:, lanes] + back
        if b == 1:
            @pl.when(ck == c)
            def _():
                core_copy(xk).wait_recv()
                both = macc[k] + cin[xk].astype(F32)

                @pl.when(xk == x)
                def _():
                    macc[k] = both

                @pl.when(xk != x)
                def _():
                    xsend[...] = both.astype(BF16)
                    x_copy.start()

    def ring(b, low, high):
        def sub_step(i, carry):
            s = i // 2
            k = jnp.where(i % 2 == 0, z - s, z + s)

            @pl.when((k >= 0) & (k <= last))
            def _():
                for j in range(PIECES):
                    y_copy(k, b, 1 - g, j).wait_recv()
                work(k, b, False)
            return carry

        lax.fori_loop(2 * low, 2 * high, sub_step, 0)

    def norm_step(i):
        at = head_cols(i)
        whole = att[:, at]
        scale = lax.rsqrt(jnp.mean(whole * whole, axis=-1, keepdims=True) + 1e-06)
        scaled = gh[:, at] * gain_ref[:, at]
        inner = jnp.mean(scaled * whole, axis=-1, keepdims=True) * scale * scale
        grad = ((scaled - whole * inner) * scale).astype(BF16)
        dout[:, at] = grad
        rbuf[i] = mul(q_ref[:, at], grad, TN).astype(BF16)

    def grad_step(i):
        at = head_cols(i)
        grad = dout[:, at]
        first, below = masked(grad, v_ref[:, at])
        outer = mul(grad, pbuf[i], NT)
        dq_ref[early, at] = (mul(first, k_ref[early, at], NN) + outer[:block]).astype(BF16)
        dq_ref[late, at] = (mul(below, k_ref[:, at], NN) + outer[block:]).astype(BF16)
        query = q_ref[:, at]
        kept = mul(below, query[block:], TN)
        att[early, at] = kept[:block] + mul(first, query[:block], TN)
        att[late, at] = kept[block:]
        given = mul(scores[i, late, :], grad[block:], TN)
        gh[early, at] = given[:block] + mul(scores[i, early, early], grad[:block], TN)
        gh[late, at] = given[block:]

    def suffix_start(low, high):
        @pl.when(z == last)
        def _():
            for i in range(low, high):
                r_copy(i, rbuf).start()

    def suffix_pass(low, high):
        @pl.when(z < last)
        def _():
            for i in range(low, high):
                r_copy(i, gsend).wait_recv()

                @pl.when(z > 0)
                def _():
                    at = pl.ds(i * part, part)
                    gsend[at] = (rbuf[at].astype(F32) + gbuf[at].astype(F32)).astype(BF16)
                    r_copy(i, gsend).start()

    def last_step(i):
        at = head_cols(i)
        dk_ref[:, at] = (att[:, at] + mul(v_ref[:, at], gbuf[i], NT)).astype(BF16)
        dv_ref[:, at] = (gh[:, at] + mul(k_ref[:, at], gbuf[i], NN)).astype(BF16)

    @pl.when(z == last)
    def _():
        gbuf[...] = jnp.zeros_like(gbuf)

    work(z, 0, True)
    ring(0, 1, 3)
    pass_on(0, 3)
    ring(0, 3, 4)
    pass_on(1, 1)
    for_heads(0, mid, norm_step)
    suffix_start(0, SPANS // 2)
    pass_on(1, 2)
    for_heads(0, mid, grad_step)
    work(z, 1, True)
    ring(1, 1, 2)
    pass_on(1, 3)
    ring(1, 2, 3)
    suffix_pass(0, SPANS // 2)
    ring(1, 3, 4)
    for_heads(mid, heads, norm_step)
    suffix_start(SPANS // 2, SPANS)
    for_heads(0, mid, last_step)
    for_heads(mid, heads, grad_step)
    suffix_pass(SPANS // 2, SPANS)
    for_heads(mid, heads, last_step)

    x_copy.wait_recv()
    mixed_ref[...] = (macc[h] + xin[...].astype(F32)).astype(BF16)

    og_core.wait_send()
    og_x.wait_send()
    og_forward.wait_send()
    x_copy.wait_send()
    for xk in range(2):
        core_copy(xk).wait_send()
    for i in range(SPANS):
        pl.when(z < last)(lambda i=i: p_copy(i, sbuf).wait_send())
        pl.when(z > 0)(lambda i=i: r_copy(i, rbuf).wait_send())
    for k in range(4):
        for b in range(2):
            for j in range(PIECES):
                pl.when((z >= k) & (z < last))(lambda: up_copy(k, b, j).wait_send())
                pl.when((z <= k) & (z > 0))(lambda: down_copy(k, b, j).wait_send())
                pl.when(z != k)(lambda: y_copy(k, b, g, j).wait_send())


def on_device_fused(queries, key_rows, value_rows, norm_gain, out_weight, out_grad):
    rows, width = queries.shape
    heads = width // HD
    share = out_weight.shape[1]
    inside = pl.BlockSpec(memory_space=pltpu.VMEM)
    anywhere = pl.BlockSpec(memory_space=pl.ANY)
    grid_of = jax.ShapeDtypeStruct((rows, width), BF16)
    dma = pltpu.SemaphoreType.DMA
    states = pltpu.VMEM((heads, HD, HD), BF16)
    return pl.pallas_call(
        fused_kernel,
        out_shape=(jax.ShapeDtypeStruct((rows, share), BF16), grid_of, grid_of, grid_of),
        in_specs=[inside] * 4 + [anywhere] * 2,
        out_specs=(inside,) * 4,
        scratch_shapes=[
            pltpu.VMEM((4, 2, width // 2, share), BF16),
            pltpu.VMEM((4, rows, share), BF16),
            pltpu.VMEM((rows, width), F32),
            pltpu.VMEM((rows, width), F32),
            pltpu.VMEM((heads, rows, rows), BF16),
            pltpu.VMEM((rows, width), BF16),
            pltpu.VMEM((rows, width), BF16),
            pltpu.VMEM((4, rows, share), F32),
            pltpu.VMEM((2, rows, share), BF16),
            pltpu.VMEM((2, rows, share), BF16),
            pltpu.VMEM((rows, share), BF16),
            pltpu.VMEM((rows, share), BF16),
            states, states, states, states, states, states,
            dma((3,)),
            dma((4, 2, PIECES)), dma((4, 2, PIECES)), dma((4, 2, PIECES)), dma((4, 2, PIECES)), dma((4, 2, PIECES)),
            dma((3,)), dma((3,)),
            dma((SPANS,)), dma((SPANS,)), dma((SPANS,)), dma((SPANS,)),
            dma((2,)), dma((2,)), dma((1,)), dma((1,)),
        ],
        compiler_params=pltpu.CompilerParams(
            collective_id=0, has_side_effects=True, vmem_limit_bytes=56 * 1024 * 1024
        ),
        cost_estimate=pl.CostEstimate(flops=12 * 10**9, bytes_accessed=10**7, transcendentals=rows * heads),
    )(queries, key_rows, value_rows, norm_gain.reshape(1, width), out_weight, out_grad)


def solution(mesh):
    placed = (
        P(("groups", "ctx"), "head"),
        P(("groups", "ctx"), "head"),
        P(("groups", "ctx"), "head"),
        P("head"),
        P("head", "ctx"),
        P(("groups", "ctx"), "head"),
    )
    fused = all(mesh.shape[name] == size for name, size in MESH_OF_KERNEL.items())
    return jax.shard_map(
        on_device_fused if fused else on_device,
        mesh=mesh,
        in_specs=placed,
        out_specs=(
            P(("groups", "ctx"), "head"),
            P(("groups", "ctx"), "head"),
            P(("groups", "ctx"), "head"),
            P(("groups", "ctx"), "head"),
        ),
        check_vma=False,
    )
```

```python
import jax
import jax.numpy as jnp
from jax import lax
from jax.experimental import pallas as pl
from jax.experimental.pallas import tpu as pltpu
from jax.sharding import PartitionSpec as P

HD = 128


def normed(attended, gain_grid):
    meansq = jnp.mean(attended * attended, axis=-1, keepdims=True)
    return attended * lax.rsqrt(meansq + 1e-06) * gain_grid


def on_device(queries, key_rows, value_rows, norm_gain, out_weight, out_grad):
    rows = queries.shape[0]
    heads_here = queries.shape[1] // HD
    query_loc = queries.reshape(rows, heads_here, HD)
    key_loc = key_rows.reshape(rows, heads_here, HD)
    value_loc = value_rows.reshape(rows, heads_here, HD)
    gain_grid = norm_gain.reshape(heads_here, HD)
    position = lax.axis_index("ctx")
    blocks = lax.axis_size("ctx")
    order = jnp.arange(blocks)
    causal = jnp.tril(jnp.ones((rows, rows), dtype=bool))
    states = jnp.einsum(
        "lhe,lhf->hef", key_loc, value_loc, preferred_element_type=jnp.float32
    ).astype(jnp.bfloat16)
    gathered = lax.all_gather(states[None], "ctx", axis=0, tiled=True)
    earlier_mask = order < position
    prefix = jnp.sum(
        jnp.where(earlier_mask[:, None, None, None], gathered.astype(jnp.float32), 0.0), axis=0
    )
    prefix_low = prefix.astype(jnp.bfloat16)
    raw_scores = jnp.einsum("lhe,mhe->hlm", query_loc, key_loc, preferred_element_type=jnp.float32)
    scores = jnp.where(causal, raw_scores, 0.0).astype(jnp.bfloat16)
    attended = jnp.einsum("lhe,hef->lhf", query_loc, prefix_low, preferred_element_type=jnp.float32)
    attended = attended + jnp.einsum(
        "hlm,mhf->lhf", scores, value_loc, preferred_element_type=jnp.float32
    )
    hidden = normed(attended, gain_grid).astype(jnp.bfloat16).reshape(rows, heads_here * HD)
    full_weight = lax.all_gather(out_weight, "ctx", axis=1, tiled=True)
    partial_value = jnp.dot(hidden, full_weight, preferred_element_type=jnp.float32)
    mixed = lax.psum_scatter(
        partial_value.astype(jnp.bfloat16), "head", scatter_dimension=1, tiled=True
    )
    grad_cols = lax.all_gather(out_grad, "head", axis=1, tiled=True)
    grad_hidden = lax.dot_general(
        grad_cols, full_weight, (((1,), (1,)), ((), ())), preferred_element_type=jnp.float32
    )
    grad_hidden = grad_hidden.reshape(rows, heads_here, HD)
    _, pullback = jax.vjp(lambda values_in: normed(values_in, gain_grid), attended)
    grad_attended = pullback(grad_hidden)[0].astype(jnp.bfloat16)
    grad_state = jnp.einsum(
        "lhe,lhf->hef", query_loc, grad_attended, preferred_element_type=jnp.float32
    ).astype(jnp.bfloat16)
    gathered_grads = lax.all_gather(grad_state[None], "ctx", axis=0, tiled=True)
    later_mask = order > position
    suffix = jnp.sum(
        jnp.where(later_mask[:, None, None, None], gathered_grads.astype(jnp.float32), 0.0), axis=0
    )
    suffix_low = suffix.astype(jnp.bfloat16)
    raw_grad = jnp.einsum(
        "lhf,mhf->hlm", grad_attended, value_loc, preferred_element_type=jnp.float32
    )
    grad_scores = jnp.where(causal, raw_grad, 0.0).astype(jnp.bfloat16)
    query_grad = jnp.einsum(
        "hlm,mhe->lhe", grad_scores, key_loc, preferred_element_type=jnp.float32
    )
    query_grad = query_grad + jnp.einsum(
        "lhf,hef->lhe", grad_attended, prefix_low, preferred_element_type=jnp.float32
    )
    key_grad = jnp.einsum(
        "hlm,lhe->mhe", grad_scores, query_loc, preferred_element_type=jnp.float32
    )
    key_grad = key_grad + jnp.einsum(
        "mhf,hef->mhe", value_loc, suffix_low, preferred_element_type=jnp.float32
    )
    value_grad = jnp.einsum(
        "hlm,lhf->mhf", scores, grad_attended, preferred_element_type=jnp.float32
    )
    value_grad = value_grad + jnp.einsum(
        "mhe,hef->mhf", key_loc, suffix_low, preferred_element_type=jnp.float32
    )
    flat = (rows, heads_here * HD)
    return (
        mixed,
        query_grad.reshape(flat).astype(jnp.bfloat16),
        key_grad.reshape(flat).astype(jnp.bfloat16),
        value_grad.reshape(flat).astype(jnp.bfloat16),
    )


MESH_OF_KERNEL = {"groups": 2, "ctx": 4, "head": 4}
PIECES = 3
SPANS = 4
F32 = jnp.float32
BF16 = jnp.bfloat16
NN = (((1,), (0,)), ((), ()))
NT = (((1,), (1,)), ((), ()))
TN = (((0,), (0,)), ((), ()))


def mul(a, b, dims):
    return lax.dot_general(a, b, dims, preferred_element_type=F32)


def fused_kernel(
    q_ref, k_ref, v_ref, gain_ref, w_ref, og_ref,
    mixed_ref, dq_ref, dk_ref, dv_ref,
    wall, ogall, att, gh, scores, hid, dout,
    macc, csend, cin, xsend, xin, sbuf, pbuf, psend, rbuf, gbuf, gsend,
    local_sem, up_sem, down_sem, z_sem, ysend_sem, yrecv_sem, ogsend_sem, ogrecv_sem,
    psend_sem, precv_sem, rsend_sem, rrecv_sem, csend_sem, crecv_sem, xsend_sem, xrecv_sem,
):
    rows = q_ref.shape[0]
    heads = q_ref.shape[1] // HD
    half_cols = w_ref.shape[1] // 2
    piece = half_cols // PIECES
    band = wall.shape[2]
    mid = heads // 2
    part = heads // SPANS
    g = lax.axis_index("groups")
    z = lax.axis_index("ctx")
    h = lax.axis_index("head")
    last = 3
    x, c = h // 2, h % 2
    to_up, to_down = {"ctx": z + 1}, {"ctx": z - 1}
    to_y = {"groups": 1 - g}
    to_core = {"head": x * 2 + 1 - c}
    to_x = {"head": (1 - x) * 2 + c}

    def remote(src, dst, send, recv, to):
        return pltpu.make_async_remote_copy(
            src_ref=src, dst_ref=dst, send_sem=send, recv_sem=recv,
            device_id=to, device_id_type=pl.DeviceIdType.MESH,
        )

    barrier = pltpu.get_barrier_semaphore()

    def greet(to):
        pl.semaphore_signal(barrier, inc=1, device_id=to, device_id_type=pl.DeviceIdType.MESH)

    greet(to_y)
    greet(to_core)
    greet(to_x)
    pl.when(z < last)(lambda: greet(to_up))
    pl.when(z > 0)(lambda: greet(to_down))
    pl.semaphore_wait(barrier, 3 + jnp.where(z < last, 1, 0) + jnp.where(z > 0, 1, 0))

    def cols(index, width):
        if isinstance(index, int):
            return slice(index * width, (index + 1) * width)
        return pl.ds(pl.multiple_of(index * width, HD), width)

    def head_cols(index):
        return cols(index, HD)

    def w_piece(k, b, half, j):
        return wall.at[k, b, :, cols(half * PIECES + j, piece)]

    def own_piece(b, j):
        return w_ref.at[b * band:(b + 1) * band, cols(g * PIECES + j, piece)]

    def z_copy(src, k, b, j, send, to):
        return remote(src, w_piece(k, b, g, j), send.at[k, b, j], z_sem.at[k, b, j], to)

    def up_copy(k, b, j, src=None):
        return z_copy(w_piece(k, b, g, j) if src is None else src, k, b, j, up_sem, to_up)

    def down_copy(k, b, j, src=None):
        return z_copy(w_piece(k, b, g, j) if src is None else src, k, b, j, down_sem, to_down)

    def y_copy(k, b, half, j):
        return remote(
            w_piece(k, b, half, j), w_piece(k, b, half, j), ysend_sem.at[k, b, j], yrecv_sem.at[k, b, j], to_y
        )

    def og_copy(slot, index, src, to):
        return remote(src, ogall.at[slot], ogsend_sem.at[index], ogrecv_sem.at[index], to)

    og_core = og_copy(h, 0, og_ref, to_core)
    og_x = og_copy(h, 1, og_ref, to_x)
    across = (1 - x) * 2 + c
    og_forward = og_copy(across, 2, ogall.at[across], to_core)
    own_og = pltpu.make_async_copy(og_ref, ogall.at[h], local_sem.at[2])
    own_w = [
        pltpu.make_async_copy(w_ref.at[i * band:(i + 1) * band], wall.at[z, i], local_sem.at[i])
        for i in range(2)
    ]

    def send_own(b):
        for j in range(PIECES):
            pl.when(z < last)(lambda j=j: up_copy(z, b, j, own_piece(b, j)).start())
            pl.when(z > 0)(lambda j=j: down_copy(z, b, j, own_piece(b, j)).start())

    def for_heads(low, high, step):
        for i in range(low, high):
            step(i)

    send_own(0)
    og_x.start()
    og_core.start()
    own_og.start()
    for copy in own_w:
        copy.start()

    def span(ref, i):
        return ref.at[pl.ds(i * part, part)]

    def p_copy(i, src):
        return remote(span(src, i), span(pbuf, i), psend_sem.at[i], precv_sem.at[i], to_up)

    def r_copy(i, src):
        return remote(span(src, i), span(gbuf, i), rsend_sem.at[i], rrecv_sem.at[i], to_down)

    def state_step(i):
        sbuf[i] = mul(k_ref[:, head_cols(i)], v_ref[:, head_cols(i)], TN).astype(BF16)

    for_heads(0, heads, state_step)

    @pl.when(z == 0)
    def _():
        for i in range(SPANS):
            p_copy(i, sbuf).start()
        pbuf[...] = jnp.zeros_like(pbuf)

    block = rows // 2
    causal = lax.broadcasted_iota(jnp.int32, (block, block), 0) >= lax.broadcasted_iota(jnp.int32, (block, block), 1)
    early, late = slice(0, block), slice(block, rows)

    def masked(left, right):
        first = jnp.where(causal, mul(left[:block], right[:block], NT), 0.0).astype(BF16)
        cross = mul(left[block:], right[:block], NT).astype(BF16)
        second = jnp.where(causal, mul(left[block:], right[block:], NT), 0.0).astype(BF16)
        return first, jnp.concatenate([cross, second], axis=1)

    def score_step(i):
        at = head_cols(i)
        first, below = masked(q_ref[:, at], k_ref[:, at])
        scores[i, early, early] = first
        scores[i, late, :] = below
        att[early, at] = mul(first, v_ref[early, at], NN)
        att[late, at] = mul(below, v_ref[:, at], NN)

    def pass_on(b, s):
        for j in range(PIECES):
            @pl.when(z - s >= 0)
            def _():
                k = z - s
                up_copy(k, b, j).wait_recv()
                y_copy(k, b, g, j).start()
                pl.when(z < last)(lambda: up_copy(k, b, j).start())

            @pl.when(z + s <= last)
            def _():
                k = z + s
                down_copy(k, b, j).wait_recv()
                y_copy(k, b, g, j).start()
                pl.when(z > 0)(lambda: down_copy(k, b, j).start())

    for_heads(0, mid, score_step)
    pass_on(0, 1)
    for_heads(mid, heads, score_step)
    og_copy(across, 1, og_ref, to_x).wait_recv()
    og_forward.start()
    pass_on(0, 2)

    @pl.when(z > 0)
    def _():
        for i in range(SPANS):
            p_copy(i, psend).wait_recv()

            @pl.when(z < last)
            def _():
                at = pl.ds(i * part, part)
                psend[at] = (sbuf[at].astype(F32) + pbuf[at].astype(F32)).astype(BF16)
                p_copy(i, psend).start()

    send_own(1)

    def hidden_step(i):
        at = head_cols(i)
        whole = att[:, at] + mul(q_ref[:, at], pbuf[i], NN)
        att[:, at] = whole
        scale = lax.rsqrt(jnp.mean(whole * whole, axis=-1, keepdims=True) + 1e-06)
        hid[:, at] = (whole * scale * gain_ref[:, at]).astype(BF16)

    for_heads(0, heads, hidden_step)

    own_og.wait()
    for copy in own_w:
        copy.wait()
    og_core.wait_recv()
    og_forward.wait_recv()

    def core_copy(xk):
        return remote(csend.at[xk], cin.at[xk], csend_sem.at[xk], crecv_sem.at[xk], to_core)

    x_copy = remote(xsend, xin, xsend_sem.at[0], xrecv_sem.at[0], to_x)

    def work(k, b, opening):
        lanes = slice(b * band, (b + 1) * band)
        xk, ck = k // 2, k % 2
        weight = wall[k, b]
        term = mul(hid[:, lanes], weight, NN)
        if b == 0:
            macc[k] = term
        else:
            term = macc[k] + term

            @pl.when(ck != c)
            def _():
                csend[xk] = term.astype(BF16)
                core_copy(xk).start()

            @pl.when(ck == c)
            def _():
                macc[k] = term

        back = mul(ogall[k], weight, NT)
        gh[:, lanes] = back if opening else gh[:, lanes] + back
        if b == 1:
            @pl.when(ck == c)
            def _():
                core_copy(xk).wait_recv()
                both = macc[k] + cin[xk].astype(F32)

                @pl.when(xk == x)
                def _():
                    macc[k] = both

                @pl.when(xk != x)
                def _():
                    xsend[...] = both.astype(BF16)
                    x_copy.start()

    def ring(b, low, high):
        def sub_step(i, carry):
            s = i // 2
            k = jnp.where(i % 2 == 0, z - s, z + s)

            @pl.when((k >= 0) & (k <= last))
            def _():
                for j in range(PIECES):
                    y_copy(k, b, 1 - g, j).wait_recv()
                work(k, b, False)
            return carry

        lax.fori_loop(2 * low, 2 * high, sub_step, 0)

    def norm_step(i):
        at = head_cols(i)
        whole = att[:, at]
        scale = lax.rsqrt(jnp.mean(whole * whole, axis=-1, keepdims=True) + 1e-06)
        scaled = gh[:, at] * gain_ref[:, at]
        inner = jnp.mean(scaled * whole, axis=-1, keepdims=True) * scale * scale
        grad = ((scaled - whole * inner) * scale).astype(BF16)
        dout[:, at] = grad
        rbuf[i] = mul(q_ref[:, at], grad, TN).astype(BF16)

    def grad_step(i):
        at = head_cols(i)
        grad = dout[:, at]
        first, below = masked(grad, v_ref[:, at])
        outer = mul(grad, pbuf[i], NT)
        dq_ref[early, at] = (mul(first, k_ref[early, at], NN) + outer[:block]).astype(BF16)
        dq_ref[late, at] = (mul(below, k_ref[:, at], NN) + outer[block:]).astype(BF16)
        query = q_ref[:, at]
        kept = mul(below, query[block:], TN)
        att[early, at] = kept[:block] + mul(first, query[:block], TN)
        att[late, at] = kept[block:]
        given = mul(scores[i, late, :], grad[block:], TN)
        gh[early, at] = given[:block] + mul(scores[i, early, early], grad[:block], TN)
        gh[late, at] = given[block:]

    def suffix_start(low, high):
        @pl.when(z == last)
        def _():
            for i in range(low, high):
                r_copy(i, rbuf).start()

    def suffix_pass(low, high):
        @pl.when(z < last)
        def _():
            for i in range(low, high):
                r_copy(i, gsend).wait_recv()

                @pl.when(z > 0)
                def _():
                    at = pl.ds(i * part, part)
                    gsend[at] = (rbuf[at].astype(F32) + gbuf[at].astype(F32)).astype(BF16)
                    r_copy(i, gsend).start()

    def last_step(i):
        at = head_cols(i)
        dk_ref[:, at] = (att[:, at] + mul(v_ref[:, at], gbuf[i], NT)).astype(BF16)
        dv_ref[:, at] = (gh[:, at] + mul(k_ref[:, at], gbuf[i], NN)).astype(BF16)

    @pl.when(z == last)
    def _():
        gbuf[...] = jnp.zeros_like(gbuf)

    work(z, 0, True)
    ring(0, 1, 3)
    pass_on(0, 3)
    ring(0, 3, 4)
    pass_on(1, 1)
    for_heads(0, mid, norm_step)
    suffix_start(0, SPANS // 2)
    pass_on(1, 2)
    for_heads(0, mid, grad_step)
    work(z, 1, True)
    ring(1, 1, 2)
    pass_on(1, 3)
    ring(1, 2, 3)
    suffix_pass(0, SPANS // 2)
    ring(1, 3, 4)
    for_heads(mid, heads, norm_step)
    suffix_start(SPANS // 2, SPANS)
    for_heads(0, mid, last_step)
    for_heads(mid, heads, grad_step)
    suffix_pass(SPANS // 2, SPANS)
    for_heads(mid, heads, last_step)

    x_copy.wait_recv()
    mixed_ref[...] = (macc[h] + xin[...].astype(F32)).astype(BF16)

    og_core.wait_send()
    og_x.wait_send()
    og_forward.wait_send()
    x_copy.wait_send()
    for xk in range(2):
        core_copy(xk).wait_send()
    for i in range(SPANS):
        pl.when(z < last)(lambda i=i: p_copy(i, sbuf).wait_send())
        pl.when(z > 0)(lambda i=i: r_copy(i, rbuf).wait_send())
    for k in range(4):
        for b in range(2):
            for j in range(PIECES):
                pl.when((z >= k) & (z < last))(lambda: up_copy(k, b, j).wait_send())
                pl.when((z <= k) & (z > 0))(lambda: down_copy(k, b, j).wait_send())
                pl.when(z != k)(lambda: y_copy(k, b, g, j).wait_send())


def on_device_fused(queries, key_rows, value_rows, norm_gain, out_weight, out_grad):
    rows, width = queries.shape
    heads = width // HD
    share = out_weight.shape[1]
    inside = pl.BlockSpec(memory_space=pltpu.VMEM)
    anywhere = pl.BlockSpec(memory_space=pl.ANY)
    grid_of = jax.ShapeDtypeStruct((rows, width), BF16)
    dma = pltpu.SemaphoreType.DMA
    states = pltpu.VMEM((heads, HD, HD), BF16)
    return pl.pallas_call(
        fused_kernel,
        out_shape=(jax.ShapeDtypeStruct((rows, share), BF16), grid_of, grid_of, grid_of),
        in_specs=[inside] * 4 + [anywhere] * 2,
        out_specs=(inside,) * 4,
        scratch_shapes=[
            pltpu.VMEM((4, 2, width // 2, share), BF16),
            pltpu.VMEM((4, rows, share), BF16),
            pltpu.VMEM((rows, width), F32),
            pltpu.VMEM((rows, width), F32),
            pltpu.VMEM((heads, rows, rows), BF16),
            pltpu.VMEM((rows, width), BF16),
            pltpu.VMEM((rows, width), BF16),
            pltpu.VMEM((4, rows, share), F32),
            pltpu.VMEM((2, rows, share), BF16),
            pltpu.VMEM((2, rows, share), BF16),
            pltpu.VMEM((rows, share), BF16),
            pltpu.VMEM((rows, share), BF16),
            states, states, states, states, states, states,
            dma((3,)),
            dma((4, 2, PIECES)), dma((4, 2, PIECES)), dma((4, 2, PIECES)), dma((4, 2, PIECES)), dma((4, 2, PIECES)),
            dma((3,)), dma((3,)),
            dma((SPANS,)), dma((SPANS,)), dma((SPANS,)), dma((SPANS,)),
            dma((2,)), dma((2,)), dma((1,)), dma((1,)),
        ],
        compiler_params=pltpu.CompilerParams(
            collective_id=0, has_side_effects=True, vmem_limit_bytes=56 * 1024 * 1024
        ),
        cost_estimate=pl.CostEstimate(flops=12 * 10**9, bytes_accessed=10**7, transcendentals=rows * heads),
    )(queries, key_rows, value_rows, norm_gain.reshape(1, width), out_weight, out_grad)


def solution(mesh):
    placed = (
        P(("groups", "ctx"), "head"),
        P(("groups", "ctx"), "head"),
        P(("groups", "ctx"), "head"),
        P("head"),
        P("head", "ctx"),
        P(("groups", "ctx"), "head"),
    )
    fused = all(mesh.shape[name] == size for name, size in MESH_OF_KERNEL.items())
    return jax.shard_map(
        on_device_fused if fused else on_device,
        mesh=mesh,
        in_specs=placed,
        out_specs=(
            P(("groups", "ctx"), "head"),
            P(("groups", "ctx"), "head"),
            P(("groups", "ctx"), "head"),
            P(("groups", "ctx"), "head"),
        ),
        check_vma=False,
    )
```
